256 devices in a mesh: shard: 64 (over z, x, core), rep: 4 (over y).
Axes of the slice: x: 4, y: 4, z: 8, core: 2. Of those that a mesh axis runs over, the one named last changes fastest.
Arguments:
- embeddings: bfloat16 [131072, 1024], P(('shard', 'rep')), may hold values from -200 to 200
- doc_cluster: int32 [131072, 1], P(('shard', 'rep')), may hold values from 0 to 63; in each aligned block of 512 rows (0 to 511, 512 to 1023, ...) at most 16 rows name the same one
- doc_rank: int32 [131072], P(('shard', 'rep')), may hold values from 0 to 131071, each once
Outputs:
- best_similarity: float32 [131072], P(('shard', 'rep'))
The draws below stay inside these ranges and needn't reach their ends.
Inputs may be any that keep to these rules, and one draw needn't show every extreme that they name: `doc_cluster`: among the rows of one device no cluster is named more than 16 times, and some device names some cluster exactly 16 times. `doc_rank`: each rank is held by exactly one document.
All inputs are finite; a program needn't handle non-finite values.
Results may differ from the reference program's by a relative error of at most 0.00049.
Values may be sent and summed in bfloat16 or wider, within the bound.
A program may use at most 64 MiB of HBM per device.

```python
import math
import jax
import jax.numpy as jnp
import numpy as np
from jax import lax

D = 1024
DOC_DEV = 512
CLUSTERS = 64
SLOT = 16
DOCS = 131072
N_SHARD = 64
N_REP = 4


topic_count = 16


def draw_embeddings(key, part):
    key = jax.random.fold_in(key, 7)
    key_list = jax.random.split(key, 6)
    noise_part = jax.random.truncated_normal(key_list[0], -4.0, 4.0, (DOCS, D), jnp.float32)
    lo_weight, hi_weight = (0.2, 4.0)
    topics = jax.random.truncated_normal(key_list[1], -4.0, 4.0, (topic_count, D), jnp.float32)
    picked = jax.random.randint(key_list[3], (DOCS,), 0, topic_count)
    strength = jnp.exp(jax.random.uniform(key_list[4], (DOCS, 1), jnp.float32, math.log(lo_weight), math.log(hi_weight)))
    magnitude = jnp.exp(jax.random.uniform(key_list[5], (DOCS, 1), jnp.float32, 0.0, math.log(10.0)))
    mixture = noise_part + strength * topics[picked]
    return (magnitude * mixture).astype(jnp.bfloat16)


def assign_block(stream_key, own, number, rows, count, top, bound, lean):
    ranking = jax.random.permutation(stream_key, count)
    packed, usual = portions_of(count, rows * top, bound, lean, True), portions_of(count, rows * top, bound, lean, False)
    places = jnp.arange(count)

    def named(tallies, offset_by):
        used = int((tallies > 0).sum())
        fixed = max(1, used // 4)
        passed = fixed + (places - fixed + offset_by * (used - fixed)) % max(1, count - fixed)
        return jnp.zeros((count,), jnp.int32).at[ranking[jnp.where(places < fixed, places, passed)]].set(jnp.asarray(tallies, jnp.int32))

    tallies = jnp.where(number % 4 == 0, named(packed, number // 4), named(usual, number - number // 4 - 1))
    mixed = jax.random.permutation(jax.random.fold_in(own, 3), count)
    giver, sink = mixed[0:count // 2 * 2:2], mixed[1:count // 2 * 2:2]
    slack = jnp.minimum(tallies[giver] - 1, bound - tallies[sink]) // 2
    slack = jnp.where((giver == ranking[0]) | (sink == ranking[0]) | (tallies[sink] == 0), 0, jnp.maximum(slack, 0))
    passed = jax.random.randint(jax.random.fold_in(own, 4), (count // 2,), 0, 1 << 20) % (slack + 1)
    tallies = tallies.at[giver].add(-passed).at[sink].add(passed)
    members = jnp.searchsorted(jnp.cumsum(tallies), jnp.arange(rows * top), side="right").astype(jnp.int32)
    listing = members.reshape(top, rows).T
    listing = listing[jax.random.permutation(jax.random.fold_in(own, 1), rows)]
    offset_by = jax.random.randint(jax.random.fold_in(own, 2), (rows, 1), 0, top)
    return jnp.take_along_axis(listing, (jnp.arange(top)[None, :] + offset_by) % top, axis=1)


def portions_of(amount, total, bound, slope, full):
    portions = [(1 << 20) // math.isqrt(grade ** slope) + 1 for grade in range(1, amount + 1)]
    largest = bound if full else min(bound, max(-(-total // amount), total * portions[0] // sum(portions)))
    least = 1 if total - largest >= amount - 1 else 0
    counts, rest = [largest] + [least] * (amount - 1), total - largest - least * (amount - 1)
    while rest > 0:
        free = [i for i in range(1, amount) if counts[i] < largest] or [i for i in range(1, amount) if counts[i] < bound]
        mass, left = sum([portions[i] for i in free]), rest
        for i in free:
            addition = min(bound - counts[i], max(1, left * portions[i] // mass), rest)
            counts[i] = counts[i] + addition
            rest = rest - addition
    return np.array(counts)


def setup_inputs(seed: int = 0) -> dict:
    key_of = jax.random.split(jax.random.key(seed), 4)
    embeddings = draw_embeddings(jax.random.fold_in(key_of[3], 71), 0)
    doc_cluster_keys = jax.random.split(jax.random.fold_in(key_of[1], 1), DOCS // DOC_DEV)
    doc_cluster_turns = jax.random.permutation(jax.random.fold_in(key_of[1], 3), DOCS // DOC_DEV)
    doc_cluster = jax.vmap(lambda own, number: assign_block(jax.random.fold_in(key_of[1], 2), own, number, DOC_DEV, CLUSTERS, 1, SLOT, 2))(doc_cluster_keys, doc_cluster_turns).reshape((DOCS, 1))
    doc_rank = jax.random.permutation(key_of[2], DOCS).astype(jnp.int32)
    return {"embeddings": embeddings, "doc_cluster": doc_cluster, "doc_rank": doc_rank}


def unit_rows(embed_rows):
    values = embed_rows.astype(jnp.float32)
    scale = lax.rsqrt(lax.optimization_barrier(jnp.sum(values * values, axis=1, keepdims=True)) + 1e-06)
    return (values * scale).astype(jnp.bfloat16)

def reference(embeddings, doc_cluster, doc_rank):
    unit = unit_rows(embeddings).astype(jnp.float32)
    group_id = doc_cluster[:, 0].astype(jnp.int32)
    order = jnp.argsort(group_id, stable=True).astype(jnp.int32)
    span = N_SHARD * N_REP * SLOT
    block = min(512, DOCS)
    sorted_unit = jnp.take(unit, order, axis=0)
    sorted_group = jnp.take(group_id, order, axis=0)
    sorted_rank = jnp.take(doc_rank.astype(jnp.int32), order, axis=0)
    pad_unit = jnp.concatenate([jnp.zeros((span, D), jnp.float32), sorted_unit, jnp.zeros((span, D), jnp.float32)], axis=0)
    pad_group = jnp.concatenate([jnp.full((span,), -1, jnp.int32), sorted_group, jnp.full((span,), -1, jnp.int32)])
    pad_rank = jnp.concatenate([jnp.full((span,), -1, jnp.int32), sorted_rank, jnp.full((span,), -1, jnp.int32)])

    def per_block(index):
        begin = (index * block).astype(jnp.int32)
        here_unit = lax.dynamic_slice_in_dim(sorted_unit, begin, block, 0)
        here_group = lax.dynamic_slice_in_dim(sorted_group, begin, block, 0)
        here_rank = lax.dynamic_slice_in_dim(sorted_rank, begin, block, 0)
        near_unit = lax.dynamic_slice_in_dim(pad_unit, begin, block + 2 * span, 0)
        near_group = lax.dynamic_slice_in_dim(pad_group, begin, block + 2 * span, 0)
        near_rank = lax.dynamic_slice_in_dim(pad_rank, begin, block + 2 * span, 0)
        scores = jnp.dot(here_unit, near_unit.T, precision=lax.Precision.HIGHEST, preferred_element_type=jnp.float32)
        keep = (near_group[None, :] == here_group[:, None]) & (near_rank[None, :] < here_rank[:, None])
        return lax.optimization_barrier(jnp.max(jnp.where(keep, scores, -1.0), axis=1))
    best_sorted = lax.map(per_block, jnp.arange(DOCS // block, dtype=jnp.int32)).reshape(DOCS)
    return jnp.zeros((DOCS,), jnp.float32).at[order].set(best_sorted)
```

```python
import functools
from types import SimpleNamespace

import jax
import jax.numpy as jnp
from jax import lax
from jax.experimental import pallas as pl
from jax.experimental.pallas import tpu as pltpu
from jax.sharding import PartitionSpec as P

SIZES = dict(Z=8, X=4, Y=4, K=2, SLOT=16)
MESH = pl.DeviceIdType.MESH
NONE_RANK = 2.0e9


def make_config(Z, X, Y, K, SLOT):
    return SimpleNamespace(
        Z=Z, X=X, Y=Y, K=K, SLOT=SLOT, XY=X * Y, J=X * K, W=X * Y * SLOT, YS=Y // K,
        order=[0] + [d for i in range(1, Z // 2) for d in (i, Z - i)] + [Z // 2],
    )


def kernel(
    cfg, emb_ref, cl_ref, rank_ref, out_ref,
    unit, hot, lane_hot, sbuf, relay, rows, rs, rz, rp, rkown, rksib, rj, res, ret1, ret2,
    z_send, z_recv, rz_send, rz_recv, p_send, p_recv, p_self, rp_send, rp_recv, rp_self,
    s_send, s_recv, rks_send, rks_recv, r1_send, r1_recv, r1_self, r2_send, r2_recv,
):
    Z, X, Y, K, SLOT, XY, J, W, YS = (
        cfg.Z, cfg.X, cfg.Y, cfg.K, cfg.SLOT, cfg.XY, cfg.J, cfg.W, cfg.YS
    )
    order = cfg.order
    n_docs, width = emb_ref.shape
    held = Z * J
    shard = lax.axis_index("shard")
    y = lax.axis_index("rep")
    k = shard % K
    x = (shard // K) % X
    z = shard // (K * X)
    p = x * Y + y
    owner = (y % YS) == (x % YS)
    j_self = jnp.where(owner, x * K + y // YS, -1)

    def dev(zz, xx, yy, kk):
        return ((zz * X + xx) * K + kk, yy)

    def dev_line(distance):
        return dev((z + distance) % Z, x, y, k)

    def dev_owner(j):
        xx = j // K
        return dev(z, xx, (j % K) * YS + xx % YS, k)

    def dev_member(q):
        return dev(z, q // Y, q % Y, k)

    sibling = dev(z, x, y, 1 - k)

    barrier = pltpu.get_barrier_semaphore()

    @pl.loop(1, Z)
    def _(i):
        pl.semaphore_signal(barrier, inc=1, device_id=dev_line(i), device_id_type=MESH)

    @pl.loop(0, J)
    def _(j):
        @pl.when(j != j_self)
        def _():
            pl.semaphore_signal(barrier, inc=1, device_id=dev_owner(j), device_id_type=MESH)

    @pl.when(owner)
    def _():
        @pl.loop(0, XY)
        def _(q):
            @pl.when(q != p)
            def _():
                pl.semaphore_signal(barrier, inc=1, device_id=dev_member(q), device_id_type=MESH)

        pl.semaphore_signal(barrier, inc=1, device_id=sibling, device_id_type=MESH)

    cl = cl_ref[...]
    log_j = J.bit_length() - 1
    away = (z - (cl >> log_j)) & (Z - 1)
    step = jnp.where(away == 0, 0, jnp.where(away <= Z // 2, 2 * away - 1, 2 * (Z - away)))
    rel = step * J + (cl & (J - 1))
    member = lax.broadcasted_iota(jnp.int32, (held, n_docs), 0) == rel
    hot_f = jnp.where(member, 1.0, 0.0)
    hot_b = hot_f.astype(jnp.bfloat16)
    hot[...] = hot_b
    before = (
        lax.broadcasted_iota(jnp.int32, (n_docs, n_docs), 0)
        < lax.broadcasted_iota(jnp.int32, (n_docs, n_docs), 1)
    )
    before_b = jnp.where(before, 1.0, 0.0).astype(jnp.bfloat16)
    prefix = jnp.dot(hot_b, before_b, preferred_element_type=jnp.float32)
    seat = jnp.sum(hot_f * prefix, axis=0, keepdims=True).astype(jnp.int32)
    place = rel * SLOT + seat
    lane = p * SLOT + seat
    lane_b = jnp.where(
        lax.broadcasted_iota(jnp.int32, (W, n_docs), 0) == lane, 1.0, 0.0
    ).astype(jnp.bfloat16)
    lane_hot[...] = lane_b

    rank1 = rank_ref[...] + 1
    parts = [(rank1 & 63), ((rank1 >> 6) & 63), (rank1 >> 12)]
    stacked = jnp.concatenate(
        [(hot_f * part.astype(jnp.float32)).astype(jnp.bfloat16) for part in parts], axis=0
    )
    spread = lax.dot_general(
        stacked, lane_b, (((1,), (1,)), ((), ())), preferred_element_type=jnp.float32
    )
    rank_rows = spread[:held] + 64.0 * spread[held : 2 * held] + 4096.0 * spread[2 * held :]
    for c in range(held):
        rs[c // J, c % J] = rank_rows[c : c + 1]

    block = min(64, n_docs)

    @pl.loop(0, n_docs // block)
    def _(i):
        at = pl.ds(pl.multiple_of(i * block, block), block)
        values = emb_ref[at].astype(jnp.float32)
        scale = lax.rsqrt(jnp.sum(values * values, axis=1, keepdims=True) + 1e-06)
        unit[at] = (values * scale).astype(jnp.bfloat16)

    def pack(n):
        slots = lax.broadcasted_iota(jnp.int32, (J * SLOT, n_docs), 0) + n * J * SLOT
        pick = jnp.where(slots == place, 1.0, 0.0).astype(jnp.bfloat16)
        got = jnp.dot(pick, unit[...], preferred_element_type=jnp.float32)
        return got.astype(jnp.bfloat16).reshape(J, SLOT, width)

    pl.semaphore_wait(
        barrier, jnp.where(owner, (Z - 1) + (J - 1) + (XY - 1) + 1, (Z - 1) + J)
    )

    def rank_copy(n):
        return pltpu.make_async_remote_copy(
            src_ref=rs.at[n], dst_ref=rz.at[n], send_sem=rz_send.at[n], recv_sem=rz_recv.at[n],
            device_id=dev_line(Z - order[n]), device_id_type=MESH,
        )

    def line_copy(n):
        return pltpu.make_async_remote_copy(
            src_ref=sbuf.at[n], dst_ref=relay.at[n], send_sem=z_send.at[n], recv_sem=z_recv.at[n],
            device_id=dev_line(Z - order[n]), device_id_type=MESH,
        )

    for n in range(1, Z):
        rank_copy(n).start()
    for n in range(1, Z):
        sbuf[n] = pack(n)
        line_copy(n).start()
    relay[0] = pack(0)
    rz[0] = rs[0]

    for n in range(1, Z):
        rank_copy(n).wait_recv()

    @pl.loop(0, J)
    def _(j):
        @pl.when(j != j_self)
        def _():
            pltpu.make_async_remote_copy(
                src_ref=rz.at[:, j], dst_ref=rp.at[p], send_sem=rp_send, recv_sem=rp_recv,
                device_id=dev_owner(j), device_id_type=MESH,
            ).start()

        @pl.when(j == j_self)
        def _():
            pltpu.make_async_copy(rz.at[:, j], rp.at[p], rp_self).start()

    def wait_bytes(ref, sem):
        pltpu.make_async_copy(ref, ref, sem).wait()

    def sib_copy(n):
        return pltpu.make_async_remote_copy(
            src_ref=rows.at[n, 0], dst_ref=rows.at[n, 1], send_sem=s_send.at[n],
            recv_sem=s_recv.at[n], device_id=sibling, device_id_type=MESH,
        )

    def rank_sib_copy():
        return pltpu.make_async_remote_copy(
            src_ref=rkown, dst_ref=rksib, send_sem=rks_send, recv_sem=rks_recv,
            device_id=sibling, device_id_type=MESH,
        )

    def forward(n):
        @pl.loop(0, J)
        def _(j):
            @pl.when(j != j_self)
            def _():
                pltpu.make_async_remote_copy(
                    src_ref=relay.at[n, j], dst_ref=rows.at[n, 0, p], send_sem=p_send.at[n],
                    recv_sem=p_recv.at[n], device_id=dev_owner(j), device_id_type=MESH,
                ).start()

            @pl.when(j == j_self)
            def _():
                pltpu.make_async_copy(relay.at[n, j], rows.at[n, 0, p], p_self.at[n]).start()

    def collected(n):
        wait_bytes(rows.at[n, 0, pl.ds(0, XY - 1)], p_recv.at[n])
        wait_bytes(rows.at[n, 0, 0], p_self.at[n])
        sib_copy(n).start()

    def own_ranks():
        wait_bytes(rp.at[pl.ds(0, XY - 1)], rp_recv)
        wait_bytes(rp.at[0], rp_self)
        for n in range(Z):
            total = rp[0, n]
            for q in range(1, XY):
                total = total + rp[q, n]
            rkown[n] = jnp.where(total > 0.5, total - 1.0, NONE_RANK)
            res[n] = jnp.full((1, W), -1.0, jnp.float32)
        rank_sib_copy().start()

    def rank_columns():
        rank_sib_copy().wait_recv()
        for half, ref in enumerate((rkown, rksib)):
            lined = jnp.concatenate(
                [ref[n] for n in range(Z)] + [jnp.zeros((128 - Z, W), jnp.float32)], axis=0
            )
            turned = lined.T
            for n in range(Z):
                rj[n, pl.ds(half * W, W), :] = jnp.broadcast_to(turned[:, n : n + 1], (W, 128))

    def pairs(m, n):
        other = rows[m].reshape(K * W, width)
        mine = rows[n, 0].reshape(W, width)
        scores = lax.dot_general(
            other, mine, (((1,), (1,)), ((), ())), preferred_element_type=jnp.float32
        )
        rank_i = rkown[n]
        rank_j = rj[m]
        best = []
        lanes = min(128, W)
        for at in range(0, W, lanes):
            earlier = rank_j[:, :lanes] < rank_i[:, at : at + lanes]
            kept = jnp.where(earlier, scores[:, at : at + lanes], -1.0)
            best.append(jnp.max(kept, axis=0, keepdims=True))
        res[n] = jnp.maximum(res[n], jnp.concatenate(best, axis=1))

    def compute(n):
        sib_copy(n).wait_recv()
        pairs(n, n)
        if n > 0:
            @pl.loop(0, n)
            def _(m):
                pairs(m, n)
                pairs(n, m)

    for n in range(Z):
        if n > 0:
            line_copy(n).wait_recv()
        forward(n)

        @pl.when(owner)
        def _(n=n):
            if n == 1:
                own_ranks()
            if n >= 1:
                collected(n - 1)
            if n == 2:
                rank_columns()
            if n >= 2:
                compute(n - 2)

    @pl.when(owner)
    def _():
        collected(Z - 1)
        compute(Z - 2)
        compute(Z - 1)

        @pl.loop(0, XY)
        def _(q):
            @pl.when(q != p)
            def _():
                pltpu.make_async_remote_copy(
                    src_ref=res, dst_ref=ret1.at[j_self], send_sem=r1_send, recv_sem=r1_recv,
                    device_id=dev_member(q), device_id_type=MESH,
                ).start()

        pltpu.make_async_copy(res, ret1.at[j_self], r1_self).start()
        wait_bytes(ret1.at[pl.ds(0, J - 1)], r1_recv)
        wait_bytes(ret1.at[0], r1_self)

    @pl.when(jnp.logical_not(owner))
    def _():
        wait_bytes(ret1, r1_recv)

    def home_copy(n):
        return pltpu.make_async_remote_copy(
            src_ref=ret1.at[:, n], dst_ref=ret2.at[n], send_sem=r2_send.at[n],
            recv_sem=r2_recv.at[n], device_id=dev_line(order[n]), device_id_type=MESH,
        )

    for n in range(1, Z):
        home_copy(n).start()

    for n in range(1, Z):
        rank_copy(n).wait_send()
        line_copy(n).wait_send()

    @pl.when(owner)
    def _():
        for n in range(Z):
            wait_bytes(relay.at[n, pl.ds(0, J - 1)], p_send.at[n])
            sib_copy(n).wait_send()
        wait_bytes(rp.at[pl.ds(0, J - 1)], rp_send)
        rank_sib_copy().wait_send()
        wait_bytes(rp.at[pl.ds(0, XY - 1)], r1_send)

    @pl.when(jnp.logical_not(owner))
    def _():
        for n in range(Z):
            wait_bytes(relay.at[n], p_send.at[n])
        wait_bytes(rp.at[pl.ds(0, J)], rp_send)

    for n in range(1, Z):
        home_copy(n).wait_recv()
    table = jnp.concatenate(
        [ret1[j, 0] for j in range(J)] + [ret2[n, j] for n in range(1, Z) for j in range(J)],
        axis=0,
    )
    hi = table.astype(jnp.bfloat16)
    rest = table - hi.astype(jnp.float32)
    mid = rest.astype(jnp.bfloat16)
    low = (rest - mid.astype(jnp.float32)).astype(jnp.bfloat16)
    found = jnp.zeros((W, n_docs), jnp.float32)
    for part in (low, mid, hi):
        found = found + lax.dot_general(
            part, hot[...], (((0,), (0,)), ((), ())), preferred_element_type=jnp.float32
        )
    out_ref[...] = jnp.sum(found * lane_hot[...].astype(jnp.float32), axis=0, keepdims=True)
    for n in range(1, Z):
        home_copy(n).wait_send()


def on_device(cfg, embeddings, doc_cluster, doc_rank):
    n_docs, width = embeddings.shape
    Z, J, W, XY, SLOT, K = cfg.Z, cfg.J, cfg.W, cfg.XY, cfg.SLOT, cfg.K
    bf16, f32 = jnp.bfloat16, jnp.float32
    dma = pltpu.SemaphoreType.DMA
    best = pl.pallas_call(
        functools.partial(kernel, cfg),
        out_shape=jax.ShapeDtypeStruct((1, n_docs), f32),
        in_specs=[pl.BlockSpec(memory_space=pltpu.VMEM)] * 3,
        out_specs=pl.BlockSpec(memory_space=pltpu.VMEM),
        scratch_shapes=[
            pltpu.VMEM((n_docs, width), bf16),
            pltpu.VMEM((Z * J, n_docs), bf16),
            pltpu.VMEM((W, n_docs), bf16),
            pltpu.VMEM((Z, J, SLOT, width), bf16),
            pltpu.VMEM((Z, J, SLOT, width), bf16),
            pltpu.VMEM((Z, K, XY, SLOT, width), bf16),
            pltpu.VMEM((Z, J, 1, W), f32),
            pltpu.VMEM((Z, J, 1, W), f32),
            pltpu.VMEM((XY, Z, 1, W), f32),
            pltpu.VMEM((Z, 1, W), f32),
            pltpu.VMEM((Z, 1, W), f32),
            pltpu.VMEM((Z, K * W, 128), f32),
            pltpu.VMEM((Z, 1, W), f32),
            pltpu.VMEM((J, Z, 1, W), f32),
            pltpu.VMEM((Z, J, 1, W), f32),
            dma((Z,)), dma((Z,)), dma((Z,)), dma((Z,)),
            dma((Z,)), dma((Z,)), dma((Z,)),
            dma, dma, dma,
            dma((Z,)), dma((Z,)), dma, dma,
            dma, dma, dma,
            dma((Z,)), dma((Z,)),
        ],
        compiler_params=pltpu.CompilerParams(
            collective_id=0, has_side_effects=True, vmem_limit_bytes=48 * 2**20
        ),
    )(embeddings, doc_cluster.reshape(1, n_docs), doc_rank.reshape(1, n_docs))
    return best.reshape(n_docs)


def solution(mesh):
    cfg = make_config(**SIZES)
    placed = (P(("shard", "rep"), None), P(("shard", "rep"), None), P(("shard", "rep")))
    return jax.shard_map(
        functools.partial(on_device, cfg), mesh=mesh, in_specs=placed,
        out_specs=P(("shard", "rep")), check_vma=False,
    )
```

```python
import functools
from types import SimpleNamespace

import jax
import jax.numpy as jnp
from jax import lax
from jax.experimental import pallas as pl
from jax.experimental.pallas import tpu as pltpu
from jax.sharding import PartitionSpec as P

SIZES = dict(Z=8, X=4, Y=4, K=2, SLOT=16)
MESH = pl.DeviceIdType.MESH
NONE_RANK = 2.0e9


def make_config(Z, X, Y, K, SLOT):
    return SimpleNamespace(
        Z=Z, X=X, Y=Y, K=K, SLOT=SLOT, XY=X * Y, J=X * K, W=X * Y * SLOT, YS=Y // K, H=min(2, X * K),
        order=[0] + [d for i in range(1, Z // 2) for d in (i, Z - i)] + [Z // 2],
    )


def kernel(
    cfg, emb_hbm, cl_hbm, rank_hbm, out_ref,
    emb_ref, cl_ref, rank_ref, unit, row_hot, lane_hot, sbuf, relay, rows,
    rs, rz, rsum, rp, rkown, rksib, rj, res, msg, ret1, rback, ret2,
    in_sem, z_send, z_recv, rz_send, rz_recv, p_send, p_recv, p_self, rp_send, rp_recv, rp_self,
    s_send, s_recv, rks_send, rks_recv, r1_send, r1_recv, r1_self, r2_send, r2_recv,
):
    Z, X, Y, K, SLOT, XY, J, W, YS = (
        cfg.Z, cfg.X, cfg.Y, cfg.K, cfg.SLOT, cfg.XY, cfg.J, cfg.W, cfg.YS
    )
    order = cfg.order
    H = cfg.H
    JH = J // H
    n_docs, width = emb_ref.shape
    held = J * SLOT
    shard = lax.axis_index("shard")
    y = lax.axis_index("rep")
    k = shard % K
    x = (shard // K) % X
    z = shard // (K * X)
    p = x * Y + y
    owner = (y % YS) == (x % YS)
    j_self = jnp.where(owner, x * K + y // YS, -1)

    def dev(zz, xx, yy, kk):
        return ((zz * X + xx) * K + kk, yy)

    def dev_line(distance):
        return dev((z + distance) % Z, x, y, k)

    def dev_owner(j):
        xx = j // K
        return dev(z, xx, (j % K) * YS + xx % YS, k)

    def dev_member(q):
        return dev(z, q // Y, q % Y, k)

    sibling = dev(z, x, y, 1 - k)

    inputs = [
        pltpu.make_async_copy(src, dst, in_sem.at[i])
        for i, (src, dst) in enumerate(
            ((cl_hbm, cl_ref), (rank_hbm, rank_ref), (emb_hbm, emb_ref))
        )
    ]
    for copy in inputs:
        copy.start()

    barrier = pltpu.get_barrier_semaphore()

    @pl.loop(1, Z)
    def _(i):
        pl.semaphore_signal(barrier, inc=1, device_id=dev_line(i), device_id_type=MESH)

    @pl.loop(0, J)
    def _(j):
        @pl.when(j != j_self)
        def _():
            pl.semaphore_signal(barrier, inc=1, device_id=dev_owner(j), device_id_type=MESH)

    @pl.when(owner)
    def _():
        @pl.loop(0, XY)
        def _(q):
            @pl.when(q != p)
            def _():
                pl.semaphore_signal(barrier, inc=1, device_id=dev_member(q), device_id_type=MESH)

        pl.semaphore_signal(barrier, inc=1, device_id=sibling, device_id_type=MESH)

    inputs[0].wait()
    inputs[1].wait()
    cl = cl_ref[...]
    log_j = J.bit_length() - 1
    away = (z - (cl >> log_j)) & (Z - 1)
    step = jnp.where(away == 0, 0, jnp.where(away <= Z // 2, 2 * away - 1, 2 * (Z - away)))
    rel = step * J + (cl & (J - 1))
    member = lax.broadcasted_iota(jnp.int32, (Z * J, n_docs), 0) == rel
    hot_f = jnp.where(member, 1.0, 0.0)
    before = (
        lax.broadcasted_iota(jnp.int32, (n_docs, n_docs), 0)
        < lax.broadcasted_iota(jnp.int32, (n_docs, n_docs), 1)
    )
    prefix = jnp.dot(
        hot_f.astype(jnp.bfloat16), jnp.where(before, 1.0, 0.0).astype(jnp.bfloat16),
        preferred_element_type=jnp.float32,
    )
    seat = jnp.sum(hot_f * prefix, axis=0, keepdims=True).astype(jnp.int32)
    place = rel * SLOT + seat
    lane = (cl & (J - 1)) * SLOT + seat
    lane_b = jnp.where(
        lax.broadcasted_iota(jnp.int32, (held, n_docs), 0) == lane, 1.0, 0.0
    ).astype(jnp.bfloat16)
    lane_hot[...] = lane_b
    row_f = jnp.where(lax.broadcasted_iota(jnp.int32, (Z, n_docs), 0) == step, 1.0, 0.0)
    row_hot[...] = row_f

    rank1 = rank_ref[...] + 1
    parts = [(rank1 & 63), ((rank1 >> 6) & 63), (rank1 >> 12)]
    rank_rows = jnp.zeros((Z, held), jnp.float32)
    for weight, part in zip((1.0, 64.0, 4096.0), parts):
        rank_rows = rank_rows + weight * lax.dot_general(
            (row_f * part.astype(jnp.float32)).astype(jnp.bfloat16), lane_b,
            (((1,), (1,)), ((), ())), preferred_element_type=jnp.float32,
        )
    chunk_row = lax.broadcasted_iota(jnp.int32, (Z, held), 0)
    lane_group = lax.broadcasted_iota(jnp.int32, (Z, held), 1) // SLOT
    for n in range(Z):
        rs[n] = jnp.where(chunk_row == n, rank_rows, 0.0)

    inputs[2].wait()
    block = min(64, n_docs)

    @pl.loop(0, n_docs // block)
    def _(i):
        at = pl.ds(pl.multiple_of(i * block, block), block)
        values = emb_ref[at].astype(jnp.float32)
        scale = lax.rsqrt(jnp.sum(values * values, axis=1, keepdims=True) + 1e-06)
        unit[at] = (values * scale).astype(jnp.bfloat16)

    def pack(n):
        slots = lax.broadcasted_iota(jnp.int32, (J * SLOT, n_docs), 0) + n * J * SLOT
        pick = jnp.where(slots == place, 1.0, 0.0).astype(jnp.bfloat16)
        got = jnp.dot(pick, unit[...], preferred_element_type=jnp.float32)
        return got.astype(jnp.bfloat16).reshape(J, SLOT, width)

    def rank_copy(n):
        return pltpu.make_async_remote_copy(
            src_ref=rs.at[n], dst_ref=rz.at[n], send_sem=rz_send.at[n], recv_sem=rz_recv.at[n],
            device_id=dev_line(Z - order[n]), device_id_type=MESH,
        )

    def piece(h):
        return jnp.where(k == 0, h, H - 1 - h) * JH

    def line_copy(n, h):
        part = pl.ds(piece(h), JH)
        at = n * H + h
        return pltpu.make_async_remote_copy(
            src_ref=sbuf.at[n, part], dst_ref=relay.at[n, part], send_sem=z_send.at[at],
            recv_sem=z_recv.at[at], device_id=dev_line(Z - order[n]), device_id_type=MESH,
        )

    for n in range(1, Z):
        sbuf[n] = pack(n)
    relay[0] = pack(0)
    pl.semaphore_wait(
        barrier, jnp.where(owner, (Z - 1) + (J - 1) + (XY - 1) + 1, (Z - 1) + J)
    )

    for h in range(H):
        line_copy(1, h).start()
        line_copy(2, h).start()
    for n in range(1, Z):
        rank_copy(n).start()
    for n in range(3, Z, 2):
        for h in range(H):
            for step_n in range(n, min(n + 2, Z)):
                line_copy(step_n, h).start()

    def owner_turn(turn):
        return (x * K + y // YS + jnp.where(k == 0, turn, J - turn)) % J

    def wait_bytes(ref, sem):
        pltpu.make_async_copy(ref, ref, sem).wait()

    def sib_copy(n):
        return pltpu.make_async_remote_copy(
            src_ref=rows.at[n, 0], dst_ref=rows.at[n, 1], send_sem=s_send.at[n],
            recv_sem=s_recv.at[n], device_id=sibling, device_id_type=MESH,
        )

    def rank_sib_copy():
        return pltpu.make_async_remote_copy(
            src_ref=rkown, dst_ref=rksib, send_sem=rks_send, recv_sem=rks_recv,
            device_id=sibling, device_id_type=MESH,
        )

    def forward(n, h):
        @pl.loop(0, JH)
        def _(turn):
            j = piece(h) + (x * K + y // YS + turn) % JH

            @pl.when(j != j_self)
            def _():
                pltpu.make_async_remote_copy(
                    src_ref=relay.at[n, j], dst_ref=rows.at[n, 0, p], send_sem=p_send.at[n],
                    recv_sem=p_recv.at[n], device_id=dev_owner(j), device_id_type=MESH,
                ).start()

            @pl.when(j == j_self)
            def _():
                pltpu.make_async_copy(relay.at[n, j], rows.at[n, 0, p], p_self.at[n]).start()

    def forward_ranks():
        for n in range(1, Z):
            rank_copy(n).wait_recv()
        rsum[...] = rs[0] + sum(rz[n] for n in range(1, Z))

        @pl.loop(0, J)
        def _(turn):
            j = owner_turn(turn)

            @pl.when(j != j_self)
            def _():
                pltpu.make_async_remote_copy(
                    src_ref=rsum, dst_ref=rp.at[p], send_sem=rp_send, recv_sem=rp_recv,
                    device_id=dev_owner(j), device_id_type=MESH,
                ).start()

            @pl.when(j == j_self)
            def _():
                pltpu.make_async_copy(rsum, rp.at[p], rp_self).start()

    def collected(n):
        wait_bytes(rows.at[n, 0, pl.ds(0, XY - 1)], p_recv.at[n])
        wait_bytes(rows.at[n, 0, 0], p_self.at[n])
        sib_copy(n).start()

    groups = held // SLOT

    def own_ranks():
        wait_bytes(rp.at[pl.ds(0, XY - 1)], rp_recv)
        wait_bytes(rp.at[0], rp_self)
        for part in range(XY // groups):
            total = jnp.zeros((Z, held), jnp.float32)
            for g in range(groups):
                shift = ((g - j_self + groups) % groups) * SLOT
                turned = pltpu.roll(rp[part * groups + g], shift, 1)
                total = total + jnp.where(lane_group == g, turned, 0.0)
            rkown[:, pl.ds(part * held, held)] = jnp.where(total > 0.5, total - 1.0, NONE_RANK)
        res[...] = jnp.full((Z, W), -1.0, jnp.float32)
        rank_sib_copy().start()

    def rank_columns():
        rank_sib_copy().wait_recv()
        for half, ref in enumerate((rkown, rksib)):
            lined = jnp.concatenate(
                [ref[...], jnp.zeros((128 - Z, W), jnp.float32)], axis=0
            )
            turned = lined.T
            for n in range(Z):
                rj[n, pl.ds(half * W, W), :] = jnp.broadcast_to(turned[:, n : n + 1], (W, 128))

    def pairs(m, count, n):
        other = rows[pl.ds(m, count)].reshape(count * K * W, width)
        mine = rows[n, 0].reshape(W, width)
        scores = lax.dot_general(
            other, mine, (((1,), (1,)), ((), ())), preferred_element_type=jnp.float32
        )
        at = pl.ds(n, 1)
        rank_i = rkown[at, :]
        rank_j = rj[pl.ds(m, count)].reshape(count * K * W, 128)
        best = []
        lanes = min(128, W)
        for first in range(0, W, lanes):
            earlier = rank_j[:, :lanes] < rank_i[:, first : first + lanes]
            kept = jnp.where(earlier, scores[:, first : first + lanes], -1.0)
            best.append(jnp.max(kept, axis=0, keepdims=True))
        res[at, :] = jnp.maximum(res[at, :], jnp.concatenate(best, axis=1))

    def compute(n):
        sib_copy(n).wait_recv()
        if n > 1:
            @pl.loop(0, n // 2)
            def _(i):
                pairs(2 * i, 2, n)
                pairs(n, 1, 2 * i)
                pairs(n, 1, 2 * i + 1)
        if n % 2:
            pairs(n - 1, 2, n)
            pairs(n, 1, n - 1)
        else:
            pairs(n, 1, n)

    for n in range(Z):
        for h in range(H):
            if n > 0:
                line_copy(n, h).wait_recv()
            forward(n, h)
        if n == 0:
            forward_ranks()

        @pl.when(owner)
        def _(n=n):
            if n == 1:
                own_ranks()
            if n >= 1:
                collected(n - 1)
            if n == 2:
                rank_columns()
            if n >= 2:
                compute(n - 2)

    @pl.when(owner)
    def _():
        collected(Z - 1)
        compute(Z - 2)
        compute(Z - 1)

        for q in range(XY):
            shift = ((j_self - q) % groups) * SLOT
            half = res[:, pl.ds(q // groups * held, held)]
            msg[q] = jnp.where(lane_group == j_self, pltpu.roll(half, shift, 1), 0.0)

        @pl.loop(1, XY)
        def _(i):
            q = (p + i) % XY
            pltpu.make_async_remote_copy(
                src_ref=msg.at[q], dst_ref=ret1.at[j_self], send_sem=r1_send, recv_sem=r1_recv,
                device_id=dev_member(q), device_id_type=MESH,
            ).start()

        pltpu.make_async_copy(msg.at[p], ret1.at[j_self], r1_self).start()
        wait_bytes(ret1.at[pl.ds(0, J - 1)], r1_recv)
        wait_bytes(ret1.at[0], r1_self)

    @pl.when(jnp.logical_not(owner))
    def _():
        wait_bytes(ret1, r1_recv)

    rback[...] = sum(ret1[j] for j in range(1, J)) + ret1[0]

    def home_copy(n):
        return pltpu.make_async_remote_copy(
            src_ref=rback, dst_ref=ret2.at[n], send_sem=r2_send.at[n],
            recv_sem=r2_recv.at[n], device_id=dev_line(order[n]), device_id_type=MESH,
        )

    for n in range(1, Z):
        home_copy(n).start()

    for n in range(1, Z):
        rank_copy(n).wait_send()
        for h in range(H):
            line_copy(n, h).wait_send()

    @pl.when(owner)
    def _():
        for n in range(Z):
            wait_bytes(relay.at[n, pl.ds(0, J - 1)], p_send.at[n])
            sib_copy(n).wait_send()
        wait_bytes(rp.at[pl.ds(0, J - 1)], rp_send)
        rank_sib_copy().wait_send()
        wait_bytes(msg.at[pl.ds(0, XY - 1)], r1_send)

    @pl.when(jnp.logical_not(owner))
    def _():
        for n in range(Z):
            wait_bytes(relay.at[n], p_send.at[n])
        wait_bytes(rp.at[pl.ds(0, J)], rp_send)

    for n in range(1, Z):
        home_copy(n).wait_recv()
    table = jnp.where(chunk_row == 0, rback[...], 0.0)
    for n in range(1, Z):
        table = jnp.where(chunk_row == n, ret2[n], table)
    hi = table.astype(jnp.bfloat16).astype(jnp.float32)
    rest = table - hi
    mid = rest.astype(jnp.bfloat16).astype(jnp.float32)
    found = jnp.zeros((held, n_docs), jnp.float32)
    for part in (rest - mid, mid, hi):
        found = found + lax.dot_general(
            part.astype(jnp.bfloat16), row_hot[...].astype(jnp.bfloat16),
            (((0,), (0,)), ((), ())), preferred_element_type=jnp.float32,
        )
    out_ref[...] = jnp.sum(found * lane_hot[...].astype(jnp.float32), axis=0, keepdims=True)
    for n in range(1, Z):
        home_copy(n).wait_send()


def on_device(cfg, embeddings, doc_cluster, doc_rank):
    n_docs, width = embeddings.shape
    Z, J, W, XY, SLOT, K = cfg.Z, cfg.J, cfg.W, cfg.XY, cfg.SLOT, cfg.K
    bf16, f32 = jnp.bfloat16, jnp.float32
    dma = pltpu.SemaphoreType.DMA
    best = pl.pallas_call(
        functools.partial(kernel, cfg),
        out_shape=jax.ShapeDtypeStruct((1, n_docs), f32),
        in_specs=[pl.BlockSpec(memory_space=pl.ANY)] * 3,
        out_specs=pl.BlockSpec(memory_space=pltpu.VMEM),
        scratch_shapes=[
            pltpu.VMEM((n_docs, width), bf16),
            pltpu.VMEM((1, n_docs), jnp.int32),
            pltpu.VMEM((1, n_docs), jnp.int32),
            pltpu.VMEM((n_docs, width), bf16),
            pltpu.VMEM((Z, n_docs), f32),
            pltpu.VMEM((J * SLOT, n_docs), bf16),
            pltpu.VMEM((Z, J, SLOT, width), bf16),
            pltpu.VMEM((Z, J, SLOT, width), bf16),
            pltpu.VMEM((Z, K, XY, SLOT, width), bf16),
            pltpu.VMEM((Z, Z, J * SLOT), f32),
            pltpu.VMEM((Z, Z, J * SLOT), f32),
            pltpu.VMEM((Z, J * SLOT), f32),
            pltpu.VMEM((XY, Z, J * SLOT), f32),
            pltpu.VMEM((Z, W), f32),
            pltpu.VMEM((Z, W), f32),
            pltpu.VMEM((Z, K * W, 128), f32),
            pltpu.VMEM((Z, W), f32),
            pltpu.VMEM((XY, Z, J * SLOT), f32),
            pltpu.VMEM((J, Z, J * SLOT), f32),
            pltpu.VMEM((Z, J * SLOT), f32),
            pltpu.VMEM((Z, Z, J * SLOT), f32),
            dma((3,)),
            dma((Z * cfg.H,)), dma((Z * cfg.H,)), dma((Z,)), dma((Z,)),
            dma((Z,)), dma((Z,)), dma((Z,)),
            dma, dma, dma,
            dma((Z,)), dma((Z,)), dma, dma,
            dma, dma, dma,
            dma((Z,)), dma((Z,)),
        ],
        compiler_params=pltpu.CompilerParams(
            collective_id=0, has_side_effects=True, vmem_limit_bytes=63 * 2**20
        ),
    )(embeddings, doc_cluster.reshape(1, n_docs), doc_rank.reshape(1, n_docs))
    return best.reshape(n_docs)


def solution(mesh):
    cfg = make_config(**SIZES)
    placed = (P(("shard", "rep"), None), P(("shard", "rep"), None), P(("shard", "rep")))
    return jax.shard_map(
        functools.partial(on_device, cfg), mesh=mesh, in_specs=placed,
        out_specs=P(("shard", "rep")), check_vma=False,
    )
```

```python
import functools
from types import SimpleNamespace

import jax
import jax.numpy as jnp
from jax import lax
from jax.experimental import pallas as pl
from jax.experimental.pallas import tpu as pltpu
from jax.sharding import PartitionSpec as P

SIZES = dict(Z=8, X=4, Y=4, K=2, SLOT=16)
MESH = pl.DeviceIdType.MESH
NONE_RANK = 2.0e9


def make_config(Z, X, Y, K, SLOT):
    return SimpleNamespace(
        Z=Z, X=X, Y=Y, K=K, SLOT=SLOT, XY=X * Y, J=X * K, W=X * Y * SLOT, YS=Y // K, H=4,
        order=[0] + [d for i in range(1, Z // 2) for d in (i, Z - i)] + [Z // 2],
    )


def kernel(
    cfg, emb_hbm, cl_hbm, rank_hbm, out_ref,
    emb_ref, cl_ref, rank_ref, unit, row_hot, lane_hot, sbuf, relay, rows,
    rs, rz, rsum, rp, rkown, rksib, rj, res, msg, ret1, rback, ret2,
    in_sem, z_send, z_recv, rz_send, rz_recv, p_send, p_recv, p_self, rp_send, rp_recv, rp_self,
    s_send, s_recv, rks_send, rks_recv, r1_send, r1_recv, r1_self, r2_send, r2_recv,
):
    Z, X, Y, K, SLOT, XY, J, W, YS = (
        cfg.Z, cfg.X, cfg.Y, cfg.K, cfg.SLOT, cfg.XY, cfg.J, cfg.W, cfg.YS
    )
    order = cfg.order
    H = cfg.H
    JH = J // H
    n_docs, width = emb_ref.shape
    held = J * SLOT
    shard = lax.axis_index("shard")
    y = lax.axis_index("rep")
    k = shard % K
    x = (shard // K) % X
    z = shard // (K * X)
    p = x * Y + y
    owner = (y % YS) == (x % YS)
    j_self = jnp.where(owner, x * K + y // YS, -1)

    def dev(zz, xx, yy, kk):
        return ((zz * X + xx) * K + kk, yy)

    def dev_line(distance):
        return dev((z + distance) % Z, x, y, k)

    def dev_owner(j):
        xx = j // K
        return dev(z, xx, (j % K) * YS + xx % YS, k)

    def dev_member(q):
        return dev(z, q // Y, q % Y, k)

    sibling = dev(z, x, y, 1 - k)

    inputs = [
        pltpu.make_async_copy(src, dst, in_sem.at[i])
        for i, (src, dst) in enumerate(
            ((cl_hbm, cl_ref), (rank_hbm, rank_ref), (emb_hbm, emb_ref))
        )
    ]
    for copy in inputs:
        copy.start()

    barrier = pltpu.get_barrier_semaphore()

    @pl.loop(1, Z)
    def _(i):
        pl.semaphore_signal(barrier, inc=1, device_id=dev_line(i), device_id_type=MESH)

    @pl.loop(0, J)
    def _(j):
        @pl.when(j != j_self)
        def _():
            pl.semaphore_signal(barrier, inc=1, device_id=dev_owner(j), device_id_type=MESH)

    @pl.when(owner)
    def _():
        @pl.loop(0, XY)
        def _(q):
            @pl.when(q != p)
            def _():
                pl.semaphore_signal(barrier, inc=1, device_id=dev_member(q), device_id_type=MESH)

        pl.semaphore_signal(barrier, inc=1, device_id=sibling, device_id_type=MESH)

    inputs[0].wait()
    inputs[1].wait()
    cl = cl_ref[...]
    log_j = J.bit_length() - 1
    away = (z - (cl >> log_j)) & (Z - 1)
    step = jnp.where(away == 0, 0, jnp.where(away <= Z // 2, 2 * away - 1, 2 * (Z - away)))
    rel = step * J + (cl & (J - 1))
    member = lax.broadcasted_iota(jnp.int32, (Z * J, n_docs), 0) == rel
    hot_f = jnp.where(member, 1.0, 0.0)
    before = (
        lax.broadcasted_iota(jnp.int32, (n_docs, n_docs), 0)
        < lax.broadcasted_iota(jnp.int32, (n_docs, n_docs), 1)
    )
    prefix = jnp.dot(
        hot_f.astype(jnp.bfloat16), jnp.where(before, 1.0, 0.0).astype(jnp.bfloat16),
        preferred_element_type=jnp.float32,
    )
    seat = jnp.sum(hot_f * prefix, axis=0, keepdims=True).astype(jnp.int32)
    place = rel * SLOT + seat
    lane = (cl & (J - 1)) * SLOT + seat
    lane_b = jnp.where(
        lax.broadcasted_iota(jnp.int32, (held, n_docs), 0) == lane, 1.0, 0.0
    ).astype(jnp.bfloat16)
    lane_hot[...] = lane_b
    row_f = jnp.where(lax.broadcasted_iota(jnp.int32, (Z, n_docs), 0) == step, 1.0, 0.0)
    row_hot[...] = row_f

    rank1 = rank_ref[...] + 1
    parts = [(rank1 & 63), ((rank1 >> 6) & 63), (rank1 >> 12)]
    rank_rows = jnp.zeros((Z, held), jnp.float32)
    for weight, part in zip((1.0, 64.0, 4096.0), parts):
        rank_rows = rank_rows + weight * lax.dot_general(
            (row_f * part.astype(jnp.float32)).astype(jnp.bfloat16), lane_b,
            (((1,), (1,)), ((), ())), preferred_element_type=jnp.float32,
        )
    chunk_row = lax.broadcasted_iota(jnp.int32, (Z, held), 0)
    lane_group = lax.broadcasted_iota(jnp.int32, (Z, held), 1) // SLOT
    for n in range(Z):
        rs[n] = jnp.where(chunk_row == n, rank_rows, 0.0)

    inputs[2].wait()
    block = min(64, n_docs)

    @pl.loop(0, n_docs // block)
    def _(i):
        at = pl.ds(pl.multiple_of(i * block, block), block)
        values = emb_ref[at].astype(jnp.float32)
        scale = lax.rsqrt(jnp.sum(values * values, axis=1, keepdims=True) + 1e-06)
        unit[at] = (values * scale).astype(jnp.bfloat16)

    def pack(n):
        slots = lax.broadcasted_iota(jnp.int32, (J * SLOT, n_docs), 0) + n * J * SLOT
        pick = jnp.where(slots == place, 1.0, 0.0).astype(jnp.bfloat16)
        got = jnp.dot(pick, unit[...], preferred_element_type=jnp.float32)
        return got.astype(jnp.bfloat16).reshape(J, SLOT, width)

    def rank_copy(n):
        return pltpu.make_async_remote_copy(
            src_ref=rs.at[n], dst_ref=rz.at[n], send_sem=rz_send.at[n], recv_sem=rz_recv.at[n],
            device_id=dev_line(Z - order[n]), device_id_type=MESH,
        )

    def piece(h):
        return ((x * H // X + jnp.where(k == 0, h, H - h)) % H) * JH

    def line_copy(n, h):
        part = pl.ds(piece(h), JH)
        at = n * H + h
        return pltpu.make_async_remote_copy(
            src_ref=sbuf.at[n, part], dst_ref=relay.at[n, part], send_sem=z_send.at[at],
            recv_sem=z_recv.at[at], device_id=dev_line(Z - order[n]), device_id_type=MESH,
        )

    for n in range(1, Z):
        sbuf[n] = pack(n)
    relay[0] = pack(0)
    pl.semaphore_wait(
        barrier, jnp.where(owner, (Z - 1) + (J - 1) + (XY - 1) + 1, (Z - 1) + J)
    )

    for h in range(H):
        line_copy(1, h).start()
        line_copy(2, h).start()
    for n in range(1, Z):
        rank_copy(n).start()
    for n in range(3, Z, 2):
        for h in range(H):
            for step_n in range(n, min(n + 2, Z)):
                line_copy(step_n, h).start()

    def owner_turn(turn):
        return (x * K + y // YS + jnp.where(k == 0, turn, J - turn)) % J

    def wait_bytes(ref, sem):
        pltpu.make_async_copy(ref, ref, sem).wait()

    def sib_copy(n):
        return pltpu.make_async_remote_copy(
            src_ref=rows.at[n, 0], dst_ref=rows.at[n, 1], send_sem=s_send.at[n],
            recv_sem=s_recv.at[n], device_id=sibling, device_id_type=MESH,
        )

    def rank_sib_copy():
        return pltpu.make_async_remote_copy(
            src_ref=rkown, dst_ref=rksib, send_sem=rks_send, recv_sem=rks_recv,
            device_id=sibling, device_id_type=MESH,
        )

    def forward(n, h):
        @pl.loop(0, JH)
        def _(turn):
            j = piece(h) + (x * K + y // YS + turn) % JH

            @pl.when(j != j_self)
            def _():
                pltpu.make_async_remote_copy(
                    src_ref=relay.at[n, j], dst_ref=rows.at[n, 0, p], send_sem=p_send.at[n],
                    recv_sem=p_recv.at[n], device_id=dev_owner(j), device_id_type=MESH,
                ).start()

            @pl.when(j == j_self)
            def _():
                pltpu.make_async_copy(relay.at[n, j], rows.at[n, 0, p], p_self.at[n]).start()

    def forward_ranks():
        for n in range(1, Z):
            rank_copy(n).wait_recv()
        rsum[...] = rs[0] + sum(rz[n] for n in range(1, Z))

        @pl.loop(0, J)
        def _(turn):
            j = owner_turn(turn)

            @pl.when(j != j_self)
            def _():
                pltpu.make_async_remote_copy(
                    src_ref=rsum, dst_ref=rp.at[p], send_sem=rp_send, recv_sem=rp_recv,
                    device_id=dev_owner(j), device_id_type=MESH,
                ).start()

            @pl.when(j == j_self)
            def _():
                pltpu.make_async_copy(rsum, rp.at[p], rp_self).start()

    def collected(n):
        wait_bytes(rows.at[n, 0, pl.ds(0, XY - 1)], p_recv.at[n])
        wait_bytes(rows.at[n, 0, 0], p_self.at[n])
        sib_copy(n).start()

    groups = held // SLOT

    def own_ranks():
        wait_bytes(rp.at[pl.ds(0, XY - 1)], rp_recv)
        wait_bytes(rp.at[0], rp_self)
        for part in range(XY // groups):
            total = jnp.zeros((Z, held), jnp.float32)
            for g in range(groups):
                shift = ((g - j_self + groups) % groups) * SLOT
                turned = pltpu.roll(rp[part * groups + g], shift, 1)
                total = total + jnp.where(lane_group == g, turned, 0.0)
            rkown[:, pl.ds(part * held, held)] = jnp.where(total > 0.5, total - 1.0, NONE_RANK)
        res[...] = jnp.full((Z, W), -1.0, jnp.float32)
        rank_sib_copy().start()

    def rank_columns():
        rank_sib_copy().wait_recv()
        for half, ref in enumerate((rkown, rksib)):
            lined = jnp.concatenate(
                [ref[...], jnp.zeros((128 - Z, W), jnp.float32)], axis=0
            )
            turned = lined.T
            for n in range(Z):
                rj[n, pl.ds(half * W, W), :] = jnp.broadcast_to(turned[:, n : n + 1], (W, 128))

    def pairs(m, count, n):
        other = rows[pl.ds(m, count)].reshape(count * K * W, width)
        mine = rows[n, 0].reshape(W, width)
        scores = lax.dot_general(
            other, mine, (((1,), (1,)), ((), ())), preferred_element_type=jnp.float32
        )
        at = pl.ds(n, 1)
        rank_i = rkown[at, :]
        rank_j = rj[pl.ds(m, count)].reshape(count * K * W, 128)
        best = []
        lanes = min(128, W)
        for first in range(0, W, lanes):
            earlier = rank_j[:, :lanes] < rank_i[:, first : first + lanes]
            kept = jnp.where(earlier, scores[:, first : first + lanes], -1.0)
            best.append(jnp.max(kept, axis=0, keepdims=True))
        res[at, :] = jnp.maximum(res[at, :], jnp.concatenate(best, axis=1))

    def compute(n):
        sib_copy(n).wait_recv()
        if n > 1:
            @pl.loop(0, n // 2)
            def _(i):
                pairs(2 * i, 2, n)
                pairs(n, 1, 2 * i)
                pairs(n, 1, 2 * i + 1)
        if n % 2:
            pairs(n - 1, 2, n)
            pairs(n, 1, n - 1)
        else:
            pairs(n, 1, n)

    for n in range(Z):
        for h in range(H):
            if n > 0:
                line_copy(n, h).wait_recv()
            forward(n, h)
        if n == 0:
            forward_ranks()

        @pl.when(owner)
        def _(n=n):
            if n == 1:
                own_ranks()
            if n >= 1:
                collected(n - 1)
            if n == 2:
                rank_columns()
            if n >= 2:
                compute(n - 2)

    @pl.when(owner)
    def _():
        collected(Z - 1)
        compute(Z - 2)
        compute(Z - 1)

        for q in range(XY):
            shift = ((j_self - q) % groups) * SLOT
            half = res[:, pl.ds(q // groups * held, held)]
            msg[q] = jnp.where(lane_group == j_self, pltpu.roll(half, shift, 1), 0.0)

        @pl.loop(1, XY)
        def _(i):
            q = (p + i) % XY
            pltpu.make_async_remote_copy(
                src_ref=msg.at[q], dst_ref=ret1.at[j_self], send_sem=r1_send, recv_sem=r1_recv,
                device_id=dev_member(q), device_id_type=MESH,
            ).start()

        pltpu.make_async_copy(msg.at[p], ret1.at[j_self], r1_self).start()
        wait_bytes(ret1.at[pl.ds(0, J - 1)], r1_recv)
        wait_bytes(ret1.at[0], r1_self)

    @pl.when(jnp.logical_not(owner))
    def _():
        wait_bytes(ret1, r1_recv)

    rback[...] = sum(ret1[j] for j in range(1, J)) + ret1[0]

    def home_copy(n):
        return pltpu.make_async_remote_copy(
            src_ref=rback, dst_ref=ret2.at[n], send_sem=r2_send.at[n],
            recv_sem=r2_recv.at[n], device_id=dev_line(order[n]), device_id_type=MESH,
        )

    for n in range(1, Z):
        home_copy(n).start()

    for n in range(1, Z):
        rank_copy(n).wait_send()
        for h in range(H):
            line_copy(n, h).wait_send()

    @pl.when(owner)
    def _():
        for n in range(Z):
            wait_bytes(relay.at[n, pl.ds(0, J - 1)], p_send.at[n])
            sib_copy(n).wait_send()
        wait_bytes(rp.at[pl.ds(0, J - 1)], rp_send)
        rank_sib_copy().wait_send()
        wait_bytes(msg.at[pl.ds(0, XY - 1)], r1_send)

    @pl.when(jnp.logical_not(owner))
    def _():
        for n in range(Z):
            wait_bytes(relay.at[n], p_send.at[n])
        wait_bytes(rp.at[pl.ds(0, J)], rp_send)

    for n in range(1, Z):
        home_copy(n).wait_recv()
    table = jnp.where(chunk_row == 0, rback[...], 0.0)
    for n in range(1, Z):
        table = jnp.where(chunk_row == n, ret2[n], table)
    hi = table.astype(jnp.bfloat16).astype(jnp.float32)
    rest = table - hi
    mid = rest.astype(jnp.bfloat16).astype(jnp.float32)
    found = jnp.zeros((held, n_docs), jnp.float32)
    for part in (rest - mid, mid, hi):
        found = found + lax.dot_general(
            part.astype(jnp.bfloat16), row_hot[...].astype(jnp.bfloat16),
            (((0,), (0,)), ((), ())), preferred_element_type=jnp.float32,
        )
    out_ref[...] = jnp.sum(found * lane_hot[...].astype(jnp.float32), axis=0, keepdims=True)
    for n in range(1, Z):
        home_copy(n).wait_send()


def on_device(cfg, embeddings, doc_cluster, doc_rank):
    n_docs, width = embeddings.shape
    Z, J, W, XY, SLOT, K = cfg.Z, cfg.J, cfg.W, cfg.XY, cfg.SLOT, cfg.K
    bf16, f32 = jnp.bfloat16, jnp.float32
    dma = pltpu.SemaphoreType.DMA
    best = pl.pallas_call(
        functools.partial(kernel, cfg),
        out_shape=jax.ShapeDtypeStruct((1, n_docs), f32),
        in_specs=[pl.BlockSpec(memory_space=pl.ANY)] * 3,
        out_specs=pl.BlockSpec(memory_space=pltpu.VMEM),
        scratch_shapes=[
            pltpu.VMEM((n_docs, width), bf16),
            pltpu.VMEM((1, n_docs), jnp.int32),
            pltpu.VMEM((1, n_docs), jnp.int32),
            pltpu.VMEM((n_docs, width), bf16),
            pltpu.VMEM((Z, n_docs), f32),
            pltpu.VMEM((J * SLOT, n_docs), bf16),
            pltpu.VMEM((Z, J, SLOT, width), bf16),
            pltpu.VMEM((Z, J, SLOT, width), bf16),
            pltpu.VMEM((Z, K, XY, SLOT, width), bf16),
            pltpu.VMEM((Z, Z, J * SLOT), f32),
            pltpu.VMEM((Z, Z, J * SLOT), f32),
            pltpu.VMEM((Z, J * SLOT), f32),
            pltpu.VMEM((XY, Z, J * SLOT), f32),
            pltpu.VMEM((Z, W), f32),
            pltpu.VMEM((Z, W), f32),
            pltpu.VMEM((Z, K * W, 128), f32),
            pltpu.VMEM((Z, W), f32),
            pltpu.VMEM((XY, Z, J * SLOT), f32),
            pltpu.VMEM((J, Z, J * SLOT), f32),
            pltpu.VMEM((Z, J * SLOT), f32),
            pltpu.VMEM((Z, Z, J * SLOT), f32),
            dma((3,)),
            dma((Z * cfg.H,)), dma((Z * cfg.H,)), dma((Z,)), dma((Z,)),
            dma((Z,)), dma((Z,)), dma((Z,)),
            dma, dma, dma,
            dma((Z,)), dma((Z,)), dma, dma,
            dma, dma, dma,
            dma((Z,)), dma((Z,)),
        ],
        compiler_params=pltpu.CompilerParams(
            collective_id=0, has_side_effects=True, vmem_limit_bytes=63 * 2**20
        ),
    )(embeddings, doc_cluster.reshape(1, n_docs), doc_rank.reshape(1, n_docs))
    return best.reshape(n_docs)


def solution(mesh):
    cfg = make_config(**SIZES)
    placed = (P(("shard", "rep"), None), P(("shard", "rep"), None), P(("shard", "rep")))
    return jax.shard_map(
        functools.partial(on_device, cfg), mesh=mesh, in_specs=placed,
        out_specs=P(("shard", "rep")), check_vma=False,
    )
```

```python
import functools
from types import SimpleNamespace

import jax
import jax.numpy as jnp
from jax import lax
from jax.experimental import pallas as pl
from jax.experimental.pallas import tpu as pltpu
from jax.sharding import PartitionSpec as P

SIZES = dict(Z=8, X=4, Y=4, K=2, SLOT=16)
MESH = pl.DeviceIdType.MESH
NONE_RANK = 2.0e9


def make_config(Z, X, Y, K, SLOT):
    return SimpleNamespace(
        Z=Z, X=X, Y=Y, K=K, SLOT=SLOT, XY=X * Y, J=X * K, W=X * Y * SLOT, YS=Y // K, H=4,
        order=[0] + [d for i in range(1, Z // 2) for d in (i, Z - i)] + [Z // 2],
    )


def kernel(
    cfg, emb_hbm, cl_hbm, rank_hbm, out_ref,
    emb_ref, cl_ref, rank_ref, unit, row_hot, lane_hot, sbuf, relay, rows,
    rs, rz, rsum, rp, rkown, rksib, rj, res, msg, ret1, rback, ret2,
    in_sem, z_send, z_recv, rz_send, rz_recv, p_send, p_recv, p_self, rp_send, rp_recv, rp_self,
    s_send, s_recv, rks_send, rks_recv, r1_send, r1_recv, r1_self, r2_send, r2_recv,
):
    Z, X, Y, K, SLOT, XY, J, W, YS = (
        cfg.Z, cfg.X, cfg.Y, cfg.K, cfg.SLOT, cfg.XY, cfg.J, cfg.W, cfg.YS
    )
    order = cfg.order
    H = cfg.H
    JH = J // H
    n_docs, width = emb_ref.shape
    held = J * SLOT
    shard = lax.axis_index("shard")
    y = lax.axis_index("rep")
    k = shard % K
    x = (shard // K) % X
    z = shard // (K * X)
    p = x * Y + y
    owner = (y % YS) == (x % YS)
    j_self = jnp.where(owner, x * K + y // YS, -1)

    def dev(zz, xx, yy, kk):
        return ((zz * X + xx) * K + kk, yy)

    def dev_line(distance):
        return dev((z + distance) % Z, x, y, k)

    def dev_owner(j):
        xx = j // K
        return dev(z, xx, (j % K) * YS + xx % YS, k)

    def dev_member(q):
        return dev(z, q // Y, q % Y, k)

    sibling = dev(z, x, y, 1 - k)

    inputs = [
        pltpu.make_async_copy(src, dst, in_sem.at[i])
        for i, (src, dst) in enumerate(
            ((cl_hbm, cl_ref), (rank_hbm, rank_ref), (emb_hbm, emb_ref))
        )
    ]
    for copy in inputs:
        copy.start()

    barrier = pltpu.get_barrier_semaphore()

    @pl.loop(1, Z)
    def _(i):
        pl.semaphore_signal(barrier, inc=1, device_id=dev_line(i), device_id_type=MESH)

    @pl.loop(0, J)
    def _(j):
        @pl.when(j != j_self)
        def _():
            pl.semaphore_signal(barrier, inc=1, device_id=dev_owner(j), device_id_type=MESH)

    @pl.when(owner)
    def _():
        @pl.loop(0, XY)
        def _(q):
            @pl.when(q != p)
            def _():
                pl.semaphore_signal(barrier, inc=1, device_id=dev_member(q), device_id_type=MESH)

        pl.semaphore_signal(barrier, inc=1, device_id=sibling, device_id_type=MESH)

    inputs[0].wait()
    inputs[1].wait()
    cl = cl_ref[...]
    log_j = J.bit_length() - 1
    away = (z - (cl >> log_j)) & (Z - 1)
    step = jnp.where(away == 0, 0, jnp.where(away <= Z // 2, 2 * away - 1, 2 * (Z - away)))
    rel = step * J + (cl & (J - 1))
    member = lax.broadcasted_iota(jnp.int32, (Z * J, n_docs), 0) == rel
    hot_f = jnp.where(member, 1.0, 0.0)
    before = (
        lax.broadcasted_iota(jnp.int32, (n_docs, n_docs), 0)
        < lax.broadcasted_iota(jnp.int32, (n_docs, n_docs), 1)
    )
    prefix = jnp.dot(
        hot_f.astype(jnp.bfloat16), jnp.where(before, 1.0, 0.0).astype(jnp.bfloat16),
        preferred_element_type=jnp.float32,
    )
    seat = jnp.sum(hot_f * prefix, axis=0, keepdims=True).astype(jnp.int32)
    place = rel * SLOT + seat
    lane = (cl & (J - 1)) * SLOT + seat
    lane_b = jnp.where(
        lax.broadcasted_iota(jnp.int32, (held, n_docs), 0) == lane, 1.0, 0.0
    ).astype(jnp.bfloat16)
    lane_hot[...] = lane_b
    row_f = jnp.where(lax.broadcasted_iota(jnp.int32, (Z, n_docs), 0) == step, 1.0, 0.0)
    row_hot[...] = row_f

    rank1 = rank_ref[...] + 1
    parts = [(rank1 & 63), ((rank1 >> 6) & 63), (rank1 >> 12)]
    rank_rows = jnp.zeros((Z, held), jnp.float32)
    for weight, part in zip((1.0, 64.0, 4096.0), parts):
        rank_rows = rank_rows + weight * lax.dot_general(
            (row_f * part.astype(jnp.float32)).astype(jnp.bfloat16), lane_b,
            (((1,), (1,)), ((), ())), preferred_element_type=jnp.float32,
        )
    chunk_row = lax.broadcasted_iota(jnp.int32, (Z, held), 0)
    lane_group = lax.broadcasted_iota(jnp.int32, (Z, held), 1) // SLOT
    for n in range(Z):
        rs[n] = jnp.where(chunk_row == n, rank_rows, 0.0)

    inputs[2].wait()
    block = min(64, n_docs)

    @pl.loop(0, n_docs // block)
    def _(i):
        at = pl.ds(pl.multiple_of(i * block, block), block)
        values = emb_ref[at].astype(jnp.float32)
        scale = lax.rsqrt(jnp.sum(values * values, axis=1, keepdims=True) + 1e-06)
        unit[at] = (values * scale).astype(jnp.bfloat16)

    def pack(n):
        slots = lax.broadcasted_iota(jnp.int32, (J * SLOT, n_docs), 0) + n * J * SLOT
        pick = jnp.where(slots == place, 1.0, 0.0).astype(jnp.bfloat16)
        got = jnp.dot(pick, unit[...], preferred_element_type=jnp.float32)
        return got.astype(jnp.bfloat16).reshape(J, SLOT, width)

    def rank_copy(n):
        return pltpu.make_async_remote_copy(
            src_ref=rs.at[n], dst_ref=rz.at[n], send_sem=rz_send.at[n], recv_sem=rz_recv.at[n],
            device_id=dev_line(Z - order[n]), device_id_type=MESH,
        )

    def piece(h):
        return ((x * H // X + jnp.where(k == 0, h, H - h)) % H) * JH

    def line_copy(n, h):
        part = pl.ds(piece(h), JH)
        at = n * H + h
        return pltpu.make_async_remote_copy(
            src_ref=sbuf.at[n, part], dst_ref=relay.at[n, part], send_sem=z_send.at[at],
            recv_sem=z_recv.at[at], device_id=dev_line(Z - order[n]), device_id_type=MESH,
        )

    for n in range(1, Z):
        sbuf[n] = pack(n)
    relay[0] = pack(0)
    pl.semaphore_wait(
        barrier, jnp.where(owner, (Z - 1) + (J - 1) + (XY - 1) + 1, (Z - 1) + J)
    )

    for h in range(H):
        line_copy(1, h).start()
        line_copy(2, h).start()
    for n in range(1, Z):
        rank_copy(n).start()
    for n in range(3, Z, 2):
        for h in range(H):
            for step_n in range(n, min(n + 2, Z)):
                line_copy(step_n, h).start()

    def owner_turn(turn):
        return (x * K + y // YS + jnp.where(k == 0, turn, J - turn)) % J

    def wait_bytes(ref, sem):
        pltpu.make_async_copy(ref, ref, sem).wait()

    def sib_copy(n):
        return pltpu.make_async_remote_copy(
            src_ref=rows.at[n, 0], dst_ref=rows.at[n, 1], send_sem=s_send.at[n],
            recv_sem=s_recv.at[n], device_id=sibling, device_id_type=MESH,
        )

    def rank_sib_copy():
        return pltpu.make_async_remote_copy(
            src_ref=rkown, dst_ref=rksib, send_sem=rks_send, recv_sem=rks_recv,
            device_id=sibling, device_id_type=MESH,
        )

    def forward(n, h):
        @pl.loop(0, JH)
        def _(turn):
            j = piece(h) + (x * K + y // YS + turn) % JH

            @pl.when(j != j_self)
            def _():
                pltpu.make_async_remote_copy(
                    src_ref=relay.at[n, j], dst_ref=rows.at[n, 0, p], send_sem=p_send.at[n],
                    recv_sem=p_recv.at[n], device_id=dev_owner(j), device_id_type=MESH,
                ).start()

            @pl.when(j == j_self)
            def _():
                pltpu.make_async_copy(relay.at[n, j], rows.at[n, 0, p], p_self.at[n]).start()

    def forward_ranks():
        for n in range(1, Z):
            rank_copy(n).wait_recv()
        rsum[...] = rs[0] + sum(rz[n] for n in range(1, Z))

        @pl.loop(0, J)
        def _(turn):
            j = owner_turn(turn)

            @pl.when(j != j_self)
            def _():
                pltpu.make_async_remote_copy(
                    src_ref=rsum, dst_ref=rp.at[p], send_sem=rp_send, recv_sem=rp_recv,
                    device_id=dev_owner(j), device_id_type=MESH,
                ).start()

            @pl.when(j == j_self)
            def _():
                pltpu.make_async_copy(rsum, rp.at[p], rp_self).start()

    def collected(n):
        wait_bytes(rows.at[n, 0, pl.ds(0, XY - 1)], p_recv.at[n])
        wait_bytes(rows.at[n, 0, 0], p_self.at[n])
        sib_copy(n).start()

    groups = held // SLOT

    def own_ranks():
        wait_bytes(rp.at[pl.ds(0, XY - 1)], rp_recv)
        wait_bytes(rp.at[0], rp_self)
        for part in range(XY // groups):
            total = jnp.zeros((Z, held), jnp.float32)
            for g in range(groups):
                shift = ((g - j_self + groups) % groups) * SLOT
                turned = pltpu.roll(rp[part * groups + g], shift, 1)
                total = total + jnp.where(lane_group == g, turned, 0.0)
            rkown[:, pl.ds(part * held, held)] = jnp.where(total > 0.5, total - 1.0, NONE_RANK)
        res[...] = jnp.full((Z, W), -1.0, jnp.float32)
        rank_sib_copy().start()

    def rank_columns():
        rank_sib_copy().wait_recv()
        for half, ref in enumerate((rkown, rksib)):
            lined = jnp.concatenate(
                [ref[...], jnp.zeros((128 - Z, W), jnp.float32)], axis=0
            )
            turned = lined.T
            for n in range(Z):
                rj[n, pl.ds(half * W, W), :] = jnp.broadcast_to(turned[:, n : n + 1], (W, 128))

    def pairs(m, count, n):
        other = rows[pl.ds(m, count)].reshape(count * K * W, width)
        mine = rows[n, 0].reshape(W, width)
        scores = lax.dot_general(
            other, mine, (((1,), (1,)), ((), ())), preferred_element_type=jnp.float32
        )
        at = pl.ds(n, 1)
        rank_i = rkown[at, :]
        rank_j = rj[pl.ds(m, count)].reshape(count * K * W, 128)
        best = []
        lanes = min(128, W)
        for first in range(0, W, lanes):
            earlier = rank_j[:, :lanes] < rank_i[:, first : first + lanes]
            kept = jnp.where(earlier, scores[:, first : first + lanes], -1.0)
            best.append(jnp.max(kept, axis=0, keepdims=True))
        res[at, :] = jnp.maximum(res[at, :], jnp.concatenate(best, axis=1))

    def tasks(n):
        calls = []
        for m in range(0, n - 1, 2):
            calls += [(m, 2, n), (n, 1, m), (n, 1, m + 1)]
        calls += [(n - 1, 2, n), (n, 1, n - 1)] if n % 2 else [(n, 1, n)]
        return calls

    def compute(n, calls):
        for call in calls:
            pairs(*call)

    for n in range(Z):
        waiting = tasks(n - 3) if n >= 3 else []
        waiting = waiting[len(waiting) * 1 // 5 :]
        for h in range(H):
            if n > 0:
                line_copy(n, h).wait_recv()
            forward(n, h)
            now = waiting[h * len(waiting) // H : (h + 1) * len(waiting) // H]
            if now:
                @pl.when(owner)
                def _(n=n, now=now):
                    compute(n - 3, now)

        if n == 0:
            forward_ranks()

        @pl.when(owner)
        def _(n=n):
            if n == 1:
                own_ranks()
            if n >= 1:
                collected(n - 1)
            if n == 2:
                rank_columns()
            if n >= 2:
                sib_copy(n - 2).wait_recv()
                calls = tasks(n - 2)
                if n < Z - 1:
                    calls = calls[: len(calls) * 1 // 5]
                compute(n - 2, calls)

    @pl.when(owner)
    def _():
        collected(Z - 1)
        sib_copy(Z - 2).wait_recv()
        compute(Z - 2, tasks(Z - 2))
        sib_copy(Z - 1).wait_recv()
        compute(Z - 1, tasks(Z - 1))

        for q in range(XY):
            shift = ((j_self - q) % groups) * SLOT
            half = res[:, pl.ds(q // groups * held, held)]
            msg[q] = jnp.where(lane_group == j_self, pltpu.roll(half, shift, 1), 0.0)

        for i in range(1, XY):
            q = (p + i) % XY
            pltpu.make_async_remote_copy(
                src_ref=msg.at[q], dst_ref=ret1.at[j_self], send_sem=r1_send, recv_sem=r1_recv,
                device_id=dev_member(q), device_id_type=MESH,
            ).start()

        pltpu.make_async_copy(msg.at[p], ret1.at[j_self], r1_self).start()
        wait_bytes(ret1.at[pl.ds(0, J - 1)], r1_recv)
        wait_bytes(ret1.at[0], r1_self)

    @pl.when(jnp.logical_not(owner))
    def _():
        wait_bytes(ret1, r1_recv)

    rback[...] = sum(ret1[j] for j in range(1, J)) + ret1[0]

    def home_copy(n):
        return pltpu.make_async_remote_copy(
            src_ref=rback, dst_ref=ret2.at[n], send_sem=r2_send.at[n],
            recv_sem=r2_recv.at[n], device_id=dev_line(order[n]), device_id_type=MESH,
        )

    for n in range(1, Z):
        home_copy(n).start()

    for n in range(1, Z):
        rank_copy(n).wait_send()
        for h in range(H):
            line_copy(n, h).wait_send()

    @pl.when(owner)
    def _():
        for n in range(Z):
            wait_bytes(relay.at[n, pl.ds(0, J - 1)], p_send.at[n])
            sib_copy(n).wait_send()
        wait_bytes(rp.at[pl.ds(0, J - 1)], rp_send)
        rank_sib_copy().wait_send()
        wait_bytes(msg.at[pl.ds(0, XY - 1)], r1_send)

    @pl.when(jnp.logical_not(owner))
    def _():
        for n in range(Z):
            wait_bytes(relay.at[n], p_send.at[n])
        wait_bytes(rp.at[pl.ds(0, J)], rp_send)

    for n in range(1, Z):
        home_copy(n).wait_recv()
    table = jnp.where(chunk_row == 0, rback[...], 0.0)
    for n in range(1, Z):
        table = jnp.where(chunk_row == n, ret2[n], table)
    hi = table.astype(jnp.bfloat16).astype(jnp.float32)
    rest = table - hi
    mid = rest.astype(jnp.bfloat16).astype(jnp.float32)
    found = jnp.zeros((held, n_docs), jnp.float32)
    for part in (rest - mid, mid, hi):
        found = found + lax.dot_general(
            part.astype(jnp.bfloat16), row_hot[...].astype(jnp.bfloat16),
            (((0,), (0,)), ((), ())), preferred_element_type=jnp.float32,
        )
    out_ref[...] = jnp.sum(found * lane_hot[...].astype(jnp.float32), axis=0, keepdims=True)
    for n in range(1, Z):
        home_copy(n).wait_send()


def on_device(cfg, embeddings, doc_cluster, doc_rank):
    n_docs, width = embeddings.shape
    Z, J, W, XY, SLOT, K = cfg.Z, cfg.J, cfg.W, cfg.XY, cfg.SLOT, cfg.K
    bf16, f32 = jnp.bfloat16, jnp.float32
    dma = pltpu.SemaphoreType.DMA
    best = pl.pallas_call(
        functools.partial(kernel, cfg),
        out_shape=jax.ShapeDtypeStruct((1, n_docs), f32),
        in_specs=[pl.BlockSpec(memory_space=pl.ANY)] * 3,
        out_specs=pl.BlockSpec(memory_space=pltpu.VMEM),
        scratch_shapes=[
            pltpu.VMEM((n_docs, width), bf16),
            pltpu.VMEM((1, n_docs), jnp.int32),
            pltpu.VMEM((1, n_docs), jnp.int32),
            pltpu.VMEM((n_docs, width), bf16),
            pltpu.VMEM((Z, n_docs), f32),
            pltpu.VMEM((J * SLOT, n_docs), bf16),
            pltpu.VMEM((Z, J, SLOT, width), bf16),
            pltpu.VMEM((Z, J, SLOT, width), bf16),
            pltpu.VMEM((Z, K, XY, SLOT, width), bf16),
            pltpu.VMEM((Z, Z, J * SLOT), f32),
            pltpu.VMEM((Z, Z, J * SLOT), f32),
            pltpu.VMEM((Z, J * SLOT), f32),
            pltpu.VMEM((XY, Z, J * SLOT), f32),
            pltpu.VMEM((Z, W), f32),
            pltpu.VMEM((Z, W), f32),
            pltpu.VMEM((Z, K * W, 128), f32),
            pltpu.VMEM((Z, W), f32),
            pltpu.VMEM((XY, Z, J * SLOT), f32),
            pltpu.VMEM((J, Z, J * SLOT), f32),
            pltpu.VMEM((Z, J * SLOT), f32),
            pltpu.VMEM((Z, Z, J * SLOT), f32),
            dma((3,)),
            dma((Z * cfg.H,)), dma((Z * cfg.H,)), dma((Z,)), dma((Z,)),
            dma((Z,)), dma((Z,)), dma((Z,)),
            dma, dma, dma,
            dma((Z,)), dma((Z,)), dma, dma,
            dma, dma, dma,
            dma((Z,)), dma((Z,)),
        ],
        compiler_params=pltpu.CompilerParams(
            collective_id=0, has_side_effects=True, vmem_limit_bytes=63 * 2**20
        ),
    )(embeddings, doc_cluster.reshape(1, n_docs), doc_rank.reshape(1, n_docs))
    return best.reshape(n_docs)


def solution(mesh):
    cfg = make_config(**SIZES)
    placed = (P(("shard", "rep"), None), P(("shard", "rep"), None), P(("shard", "rep")))
    return jax.shard_map(
        functools.partial(on_device, cfg), mesh=mesh, in_specs=placed,
        out_specs=P(("shard", "rep")), check_vma=False,
    )
```

```python
import functools
from types import SimpleNamespace

import jax
import jax.numpy as jnp
from jax import lax
from jax.experimental import pallas as pl
from jax.experimental.pallas import tpu as pltpu
from jax.sharding import PartitionSpec as P

SIZES = dict(Z=8, X=4, Y=4, K=2, SLOT=16)
MESH = pl.DeviceIdType.MESH
NONE_RANK = 2.0e9


def make_config(Z, X, Y, K, SLOT):
    return SimpleNamespace(
        Z=Z, X=X, Y=Y, K=K, SLOT=SLOT, XY=X * Y, J=X * K, W=X * Y * SLOT, YS=Y // K, H=4,
        order=[0] + [d for i in range(1, Z // 2) for d in (i, Z - i)] + [Z // 2],
    )


def kernel(
    cfg, emb_hbm, cl_hbm, rank_hbm, out_ref,
    emb_ref, cl_ref, rank_ref, unit, row_hot, lane_hot, sbuf, relay, rows,
    rs, rz, rsum, rp, rkown, rksib, rj, res, msg, ret1, rback, ret2,
    in_sem, z_send, z_recv, rz_send, rz_recv, p_send, p_recv, p_self, rp_send, rp_recv, rp_self,
    s_send, s_recv, rks_send, rks_recv, r1_send, r1_recv, r1_self, r2_send, r2_recv,
):
    Z, X, Y, K, SLOT, XY, J, W, YS = (
        cfg.Z, cfg.X, cfg.Y, cfg.K, cfg.SLOT, cfg.XY, cfg.J, cfg.W, cfg.YS
    )
    order = cfg.order
    H = cfg.H
    JH = J // H
    n_docs, width = emb_ref.shape
    held = J * SLOT
    shard = lax.axis_index("shard")
    y = lax.axis_index("rep")
    k = shard % K
    x = (shard // K) % X
    z = shard // (K * X)
    p = x * Y + y
    owner = (y % YS) == (x % YS)
    j_self = jnp.where(owner, x * K + y // YS, -1)

    def dev(zz, xx, yy, kk):
        return ((zz * X + xx) * K + kk, yy)

    def dev_line(distance):
        return dev((z + distance) % Z, x, y, k)

    def dev_owner(j):
        xx = j // K
        return dev(z, xx, (j % K) * YS + xx % YS, k)

    def dev_member(q):
        return dev(z, q // Y, q % Y, k)

    sibling = dev(z, x, y, 1 - k)

    inputs = [
        pltpu.make_async_copy(src, dst, in_sem.at[i])
        for i, (src, dst) in enumerate(
            ((cl_hbm, cl_ref), (rank_hbm, rank_ref), (emb_hbm, emb_ref))
        )
    ]
    for copy in inputs:
        copy.start()

    barrier = pltpu.get_barrier_semaphore()

    @pl.loop(1, Z)
    def _(i):
        pl.semaphore_signal(barrier, inc=1, device_id=dev_line(i), device_id_type=MESH)

    @pl.loop(0, J)
    def _(j):
        @pl.when(j != j_self)
        def _():
            pl.semaphore_signal(barrier, inc=1, device_id=dev_owner(j), device_id_type=MESH)

    @pl.when(owner)
    def _():
        @pl.loop(0, XY)
        def _(q):
            @pl.when(q != p)
            def _():
                pl.semaphore_signal(barrier, inc=1, device_id=dev_member(q), device_id_type=MESH)

        pl.semaphore_signal(barrier, inc=1, device_id=sibling, device_id_type=MESH)

    inputs[0].wait()
    inputs[1].wait()
    cl = cl_ref[...]
    log_j = J.bit_length() - 1
    away = (z - (cl >> log_j)) & (Z - 1)
    step = jnp.where(away == 0, 0, jnp.where(away <= Z // 2, 2 * away - 1, 2 * (Z - away)))
    rel = step * J + (cl & (J - 1))
    member = lax.broadcasted_iota(jnp.int32, (Z * J, n_docs), 0) == rel
    hot_f = jnp.where(member, 1.0, 0.0)
    before = (
        lax.broadcasted_iota(jnp.int32, (n_docs, n_docs), 0)
        < lax.broadcasted_iota(jnp.int32, (n_docs, n_docs), 1)
    )
    prefix = jnp.dot(
        hot_f.astype(jnp.bfloat16), jnp.where(before, 1.0, 0.0).astype(jnp.bfloat16),
        preferred_element_type=jnp.float32,
    )
    seat = jnp.sum(hot_f * prefix, axis=0, keepdims=True).astype(jnp.int32)
    place = rel * SLOT + seat
    lane = (cl & (J - 1)) * SLOT + seat
    lane_b = jnp.where(
        lax.broadcasted_iota(jnp.int32, (held, n_docs), 0) == lane, 1.0, 0.0
    ).astype(jnp.bfloat16)
    lane_hot[...] = lane_b
    row_f = jnp.where(lax.broadcasted_iota(jnp.int32, (Z, n_docs), 0) == step, 1.0, 0.0)
    row_hot[...] = row_f

    rank1 = rank_ref[...] + 1
    parts = [(rank1 & 63), ((rank1 >> 6) & 63), (rank1 >> 12)]
    rank_rows = jnp.zeros((Z, held), jnp.float32)
    for weight, part in zip((1.0, 64.0, 4096.0), parts):
        rank_rows = rank_rows + weight * lax.dot_general(
            (row_f * part.astype(jnp.float32)).astype(jnp.bfloat16), lane_b,
            (((1,), (1,)), ((), ())), preferred_element_type=jnp.float32,
        )
    chunk_row = lax.broadcasted_iota(jnp.int32, (Z, held), 0)
    lane_group = lax.broadcasted_iota(jnp.int32, (Z, held), 1) // SLOT
    for n in range(Z):
        rs[n] = jnp.where(chunk_row == n, rank_rows, 0.0)

    inputs[2].wait()
    block = min(64, n_docs)

    @pl.loop(0, n_docs // block)
    def _(i):
        at = pl.ds(pl.multiple_of(i * block, block), block)
        values = emb_ref[at].astype(jnp.float32)
        scale = lax.rsqrt(jnp.sum(values * values, axis=1, keepdims=True) + 1e-06)
        unit[at] = (values * scale).astype(jnp.bfloat16)

    def pack(n):
        slots = lax.broadcasted_iota(jnp.int32, (J * SLOT, n_docs), 0) + n * J * SLOT
        pick = jnp.where(slots == place, 1.0, 0.0).astype(jnp.bfloat16)
        got = jnp.dot(pick, unit[...], preferred_element_type=jnp.float32)
        return got.astype(jnp.bfloat16).reshape(J, SLOT, width)

    def rank_copy(n):
        return pltpu.make_async_remote_copy(
            src_ref=rs.at[n], dst_ref=rz.at[n], send_sem=rz_send.at[n], recv_sem=rz_recv.at[n],
            device_id=dev_line(Z - order[n]), device_id_type=MESH,
        )

    def piece(h):
        return ((x * H // X + jnp.where(k == 0, h, H - h)) % H) * JH

    def line_copy(n, h):
        part = pl.ds(piece(h), JH)
        at = n * H + h
        return pltpu.make_async_remote_copy(
            src_ref=sbuf.at[n, part], dst_ref=relay.at[n, part], send_sem=z_send.at[at],
            recv_sem=z_recv.at[at], device_id=dev_line(Z - order[n]), device_id_type=MESH,
        )

    for n in range(1, Z):
        sbuf[n] = pack(n)
    relay[0] = pack(0)
    pl.semaphore_wait(
        barrier, jnp.where(owner, (Z - 1) + (J - 1) + (XY - 1) + 1, (Z - 1) + J)
    )

    for h in range(H):
        line_copy(1, h).start()
        line_copy(2, h).start()
    for n in range(1, Z):
        rank_copy(n).start()
    for n in range(3, Z, 2):
        for h in range(H):
            for step_n in range(n, min(n + 2, Z)):
                line_copy(step_n, h).start()

    def owner_turn(turn):
        return (x * K + y // YS + jnp.where(k == 0, turn, J - turn)) % J

    def wait_bytes(ref, sem):
        pltpu.make_async_copy(ref, ref, sem).wait()

    def sib_copy(n):
        return pltpu.make_async_remote_copy(
            src_ref=rows.at[n, 0], dst_ref=rows.at[n, 1], send_sem=s_send.at[n],
            recv_sem=s_recv.at[n], device_id=sibling, device_id_type=MESH,
        )

    def rank_sib_copy():
        return pltpu.make_async_remote_copy(
            src_ref=rkown, dst_ref=rksib, send_sem=rks_send, recv_sem=rks_recv,
            device_id=sibling, device_id_type=MESH,
        )

    def forward(n, h):
        @pl.loop(0, JH)
        def _(turn):
            j = piece(h) + (x * K + y // YS + turn) % JH

            @pl.when(j != j_self)
            def _():
                pltpu.make_async_remote_copy(
                    src_ref=relay.at[n, j], dst_ref=rows.at[n, 0, p], send_sem=p_send.at[n],
                    recv_sem=p_recv.at[n], device_id=dev_owner(j), device_id_type=MESH,
                ).start()

            @pl.when(j == j_self)
            def _():
                pltpu.make_async_copy(relay.at[n, j], rows.at[n, 0, p], p_self.at[n]).start()

    def forward_ranks():
        for n in range(1, Z):
            rank_copy(n).wait_recv()
        rsum[...] = rs[0] + sum(rz[n] for n in range(1, Z))

        @pl.loop(0, J)
        def _(turn):
            j = owner_turn(turn)

            @pl.when(j != j_self)
            def _():
                pltpu.make_async_remote_copy(
                    src_ref=rsum, dst_ref=rp.at[p], send_sem=rp_send, recv_sem=rp_recv,
                    device_id=dev_owner(j), device_id_type=MESH,
                ).start()

            @pl.when(j == j_self)
            def _():
                pltpu.make_async_copy(rsum, rp.at[p], rp_self).start()

    def collected(n):
        wait_bytes(rows.at[n, 0, pl.ds(0, XY - 1)], p_recv.at[n])
        wait_bytes(rows.at[n, 0, 0], p_self.at[n])
        sib_copy(n).start()

    groups = held // SLOT

    def own_ranks():
        wait_bytes(rp.at[pl.ds(0, XY - 1)], rp_recv)
        wait_bytes(rp.at[0], rp_self)
        for part in range(XY // groups):
            total = jnp.zeros((Z, held), jnp.float32)
            for g in range(groups):
                shift = ((g - j_self + groups) % groups) * SLOT
                turned = pltpu.roll(rp[part * groups + g], shift, 1)
                total = total + jnp.where(lane_group == g, turned, 0.0)
            rkown[:, pl.ds(part * held, held)] = jnp.where(total > 0.5, total - 1.0, NONE_RANK)
        res[...] = jnp.full((Z, W), -1.0, jnp.float32)
        rank_sib_copy().start()

    def rank_columns():
        rank_sib_copy().wait_recv()
        for half, ref in enumerate((rkown, rksib)):
            lined = jnp.concatenate(
                [ref[...], jnp.zeros((128 - Z, W), jnp.float32)], axis=0
            )
            turned = lined.T
            for n in range(Z):
                rj[n, pl.ds(half * W, W), :] = jnp.broadcast_to(turned[:, n : n + 1], (W, 128))

    def pairs(m, count, n):
        other = rows[pl.ds(m, count)].reshape(count * K * W, width)
        mine = rows[n, 0].reshape(W, width)
        scores = lax.dot_general(
            other, mine, (((1,), (1,)), ((), ())), preferred_element_type=jnp.float32
        )
        at = pl.ds(n, 1)
        rank_i = rkown[at, :]
        rank_j = rj[pl.ds(m, count)].reshape(count * K * W, 128)
        best = []
        lanes = min(128, W)
        for first in range(0, W, lanes):
            earlier = rank_j[:, :lanes] < rank_i[:, first : first + lanes]
            kept = jnp.where(earlier, scores[:, first : first + lanes], -1.0)
            best.append(jnp.max(kept, axis=0, keepdims=True))
        res[at, :] = jnp.maximum(res[at, :], jnp.concatenate(best, axis=1))

    def tasks(n):
        calls = []
        for m in range(0, n - 1, 2):
            calls += [(m, 2, n), (n, 1, m), (n, 1, m + 1)]
        calls += [(n - 1, 2, n), (n, 1, n - 1)] if n % 2 else [(n, 1, n)]
        return calls

    def compute(n, calls):
        for call in calls:
            pairs(*call)

    for n in range(Z):
        waiting = tasks(n - 3) if n >= 3 else []
        waiting = waiting[len(waiting) * 0 // 5 :]
        for h in range(H):
            if n > 0:
                line_copy(n, h).wait_recv()
            forward(n, h)
            now = waiting[h * len(waiting) // H : (h + 1) * len(waiting) // H]
            if now:
                @pl.when(owner)
                def _(n=n, now=now):
                    compute(n - 3, now)

        if n == 0:
            forward_ranks()

        @pl.when(owner)
        def _(n=n):
            if n == 1:
                own_ranks()
            if n >= 1:
                collected(n - 1)
            if n == 2:
                rank_columns()
            if n >= 2:
                sib_copy(n - 2).wait_recv()
                calls = tasks(n - 2)
                if n < Z - 1:
                    calls = calls[: len(calls) * 0 // 5]
                compute(n - 2, calls)

    @pl.when(owner)
    def _():
        collected(Z - 1)
        sib_copy(Z - 2).wait_recv()
        compute(Z - 2, tasks(Z - 2))
        sib_copy(Z - 1).wait_recv()
        compute(Z - 1, tasks(Z - 1))

        for q in range(XY):
            shift = ((j_self - q) % groups) * SLOT
            half = res[:, pl.ds(q // groups * held, held)]
            msg[q] = jnp.where(lane_group == j_self, pltpu.roll(half, shift, 1), 0.0)

        for i in range(1, XY):
            q = (p + i) % XY
            pltpu.make_async_remote_copy(
                src_ref=msg.at[q], dst_ref=ret1.at[j_self], send_sem=r1_send, recv_sem=r1_recv,
                device_id=dev_member(q), device_id_type=MESH,
            ).start()

        pltpu.make_async_copy(msg.at[p], ret1.at[j_self], r1_self).start()
        wait_bytes(ret1.at[pl.ds(0, J - 1)], r1_recv)
        wait_bytes(ret1.at[0], r1_self)

    @pl.when(jnp.logical_not(owner))
    def _():
        wait_bytes(ret1, r1_recv)

    rback[...] = sum(ret1[j] for j in range(1, J)) + ret1[0]

    def home_copy(n):
        return pltpu.make_async_remote_copy(
            src_ref=rback, dst_ref=ret2.at[n], send_sem=r2_send.at[n],
            recv_sem=r2_recv.at[n], device_id=dev_line(order[n]), device_id_type=MESH,
        )

    for n in range(1, Z):
        home_copy(n).start()

    for n in range(1, Z):
        rank_copy(n).wait_send()
        for h in range(H):
            line_copy(n, h).wait_send()

    @pl.when(owner)
    def _():
        for n in range(Z):
            wait_bytes(relay.at[n, pl.ds(0, J - 1)], p_send.at[n])
            sib_copy(n).wait_send()
        wait_bytes(rp.at[pl.ds(0, J - 1)], rp_send)
        rank_sib_copy().wait_send()
        wait_bytes(msg.at[pl.ds(0, XY - 1)], r1_send)

    @pl.when(jnp.logical_not(owner))
    def _():
        for n in range(Z):
            wait_bytes(relay.at[n], p_send.at[n])
        wait_bytes(rp.at[pl.ds(0, J)], rp_send)

    for n in range(1, Z):
        home_copy(n).wait_recv()
    table = jnp.where(chunk_row == 0, rback[...], 0.0)
    for n in range(1, Z):
        table = jnp.where(chunk_row == n, ret2[n], table)
    hi = table.astype(jnp.bfloat16).astype(jnp.float32)
    rest = table - hi
    mid = rest.astype(jnp.bfloat16).astype(jnp.float32)
    found = jnp.zeros((held, n_docs), jnp.float32)
    for part in (rest - mid, mid, hi):
        found = found + lax.dot_general(
            part.astype(jnp.bfloat16), row_hot[...].astype(jnp.bfloat16),
            (((0,), (0,)), ((), ())), preferred_element_type=jnp.float32,
        )
    out_ref[...] = jnp.sum(found * lane_hot[...].astype(jnp.float32), axis=0, keepdims=True)
    for n in range(1, Z):
        home_copy(n).wait_send()


def on_device(cfg, embeddings, doc_cluster, doc_rank):
    n_docs, width = embeddings.shape
    Z, J, W, XY, SLOT, K = cfg.Z, cfg.J, cfg.W, cfg.XY, cfg.SLOT, cfg.K
    bf16, f32 = jnp.bfloat16, jnp.float32
    dma = pltpu.SemaphoreType.DMA
    best = pl.pallas_call(
        functools.partial(kernel, cfg),
        out_shape=jax.ShapeDtypeStruct((1, n_docs), f32),
        in_specs=[pl.BlockSpec(memory_space=pl.ANY)] * 3,
        out_specs=pl.BlockSpec(memory_space=pltpu.VMEM),
        scratch_shapes=[
            pltpu.VMEM((n_docs, width), bf16),
            pltpu.VMEM((1, n_docs), jnp.int32),
            pltpu.VMEM((1, n_docs), jnp.int32),
            pltpu.VMEM((n_docs, width), bf16),
            pltpu.VMEM((Z, n_docs), f32),
            pltpu.VMEM((J * SLOT, n_docs), bf16),
            pltpu.VMEM((Z, J, SLOT, width), bf16),
            pltpu.VMEM((Z, J, SLOT, width), bf16),
            pltpu.VMEM((Z, K, XY, SLOT, width), bf16),
            pltpu.VMEM((Z, Z, J * SLOT), f32),
            pltpu.VMEM((Z, Z, J * SLOT), f32),
            pltpu.VMEM((Z, J * SLOT), f32),
            pltpu.VMEM((XY, Z, J * SLOT), f32),
            pltpu.VMEM((Z, W), f32),
            pltpu.VMEM((Z, W), f32),
            pltpu.VMEM((Z, K * W, 128), f32),
            pltpu.VMEM((Z, W), f32),
            pltpu.VMEM((XY, Z, J * SLOT), f32),
            pltpu.VMEM((J, Z, J * SLOT), f32),
            pltpu.VMEM((Z, J * SLOT), f32),
            pltpu.VMEM((Z, Z, J * SLOT), f32),
            dma((3,)),
            dma((Z * cfg.H,)), dma((Z * cfg.H,)), dma((Z,)), dma((Z,)),
            dma((Z,)), dma((Z,)), dma((Z,)),
            dma, dma, dma,
            dma((Z,)), dma((Z,)), dma, dma,
            dma, dma, dma,
            dma((Z,)), dma((Z,)),
        ],
        compiler_params=pltpu.CompilerParams(
            collective_id=0, has_side_effects=True, vmem_limit_bytes=63 * 2**20
        ),
    )(embeddings, doc_cluster.reshape(1, n_docs), doc_rank.reshape(1, n_docs))
    return best.reshape(n_docs)


def solution(mesh):
    cfg = make_config(**SIZES)
    placed = (P(("shard", "rep"), None), P(("shard", "rep"), None), P(("shard", "rep")))
    return jax.shard_map(
        functools.partial(on_device, cfg), mesh=mesh, in_specs=placed,
        out_specs=P(("shard", "rep")), check_vma=False,
    )
```
